32 devices in a mesh: tm: 8 (over y, x, core), sens: 4 (over z).
Axes of the slice: x: 2, y: 2, z: 4, core: 2. Of those that a mesh axis runs over, the one named last changes fastest.
Arguments:
- observations: float32 [32, 4096], P('tm', 'sens'), may hold values from -6 to 6
- pattern: int32 [32, 32, 2], P('tm', 'sens'), may hold values from 0 to 3, all different within a row
- blocks: float32 [32, 128, 128], P('sens'), may hold values from -0.18 to 0.18
- sensor_precision: float32 [4096], P('sens'), may hold values from 0.25 to 4
- transition: float32 [256, 256], replicated, may hold values from -1 to 2
- process_precision: float32 [256, 256], replicated, may hold values from -1 to 100, as said below
- prior_mean: float32 [256], replicated, may hold values from -6 to 6
- prior_precision: float32 [256, 256], replicated, may hold values from -1 to 2, as said below
Outputs:
- means: float32 [32, 256], P(('tm', 'sens'))
- variances: float32 [32, 256], P(('tm', 'sens'))
The draws below stay inside these ranges and needn't reach their ends.
Inputs may be any that keep to these rules, and one draw needn't show every extreme that they name: `pattern`: each row names 2 different state blocks; every state block is named somewhere. `process_precision`: symmetric positive definite. `prior_precision`: symmetric positive definite.
All inputs are finite; a program needn't handle non-finite values.
Results may differ from the reference program's by a relative error of at most 0.0003.
Values sent between devices are 32-bit elements; how exact they have to be, the bound alone decides.
A program may use at most 128 MiB of HBM per device.

```python
import math
import jax
import jax.numpy as jnp
from jax import lax

STATE = 256
SENSORS = 4096
BLOCK_ROWS = 128
BLOCK_COLS = 64
BLOCKS_PER = 2
SENSOR_BLOCKS = 32
STATE_BLOCKS = 4
TSTEPS = 32


def draw_transition(key, part):
    key_decay, key_mixing = jax.random.split(key)
    decay = jnp.exp(jax.random.uniform(key_decay, (STATE,), jnp.float32, math.log(0.5), math.log(0.99)))
    mixing = jax.random.truncated_normal(key_mixing, -3.0, 3.0, (STATE, STATE), jnp.float32)
    return jnp.diag(decay) + mixing * (0.3 / math.sqrt(STATE))


def symmetric_draw(key, lowest, highest, spread):
    key_diag, key_noise = jax.random.split(key)
    diagonal = jnp.exp(jax.random.uniform(key_diag, (STATE,), jnp.float32, math.log(lowest), math.log(highest)))
    noise = jax.random.uniform(key_noise, (STATE, STATE), jnp.float32, -1.0, 1.0)
    return jnp.diag(diagonal) + (noise + noise.T) * (spread / STATE)


def draw_process_precision(key, part):
    return symmetric_draw(key, 1.0, 100.0, 0.45)


def draw_prior_precision(key, part):
    return symmetric_draw(key, 0.5, 2.0, 0.2)


def level_of(key, shape, shards, least, largest):
    def one(position, shards_of):
        heights = jax.random.uniform(jax.random.fold_in(jax.random.fold_in(key, 6), position), (shards_of,), jnp.float32, least / len(shards), largest / len(shards))
        return jnp.repeat(jnp.exp(heights), shape[position] // shards_of).reshape((-1,) + (1,) * (len(shape) - position - 1))

    loudness = one(*shards[0])
    for cut in shards[1:]:
        loudness = loudness * one(*cut)
    return loudness


def different_ones(key, rows, count, top, lift):
    sequence = jax.random.permutation(jax.random.fold_in(key, 1), count)
    favour = sequence
    for power in range(3):
        favour = favour * favour // count
    favour = favour * lift // count
    lots = jax.random.randint(jax.random.fold_in(key, 2), (rows, count), 0, 4096) + favour
    fixed_rows = jax.random.permutation(jax.random.fold_in(key, 3), rows)[jnp.arange(count) % rows]
    lots = jnp.where(jnp.arange(rows)[:, None] == fixed_rows[None, :], 1 << 14, lots)
    merit = lots * count + jnp.arange(count)
    return lax.top_k(merit.astype(jnp.int32), top)[1].astype(jnp.int32)


def normal_values(key, shape, scale, limit, shards=(), held_as=jnp.bfloat16):
    array = scale * jax.random.normal(key, shape, jnp.float32)
    if shards:
        array = array * level_of(key, shape, shards, -0.22, 0.18)
    return jnp.clip(array, -limit, limit).astype(held_as)


def setup_inputs(seed: int = 0) -> dict:
    streams_of = jax.random.split(jax.random.key(seed), 9)
    observations = normal_values(streams_of[0], (TSTEPS, SENSORS), 1.0, 6.0, ((0, 8), (1, 4)), jnp.float32)
    pattern = different_ones(streams_of[1], TSTEPS * SENSOR_BLOCKS, STATE_BLOCKS, BLOCKS_PER, 0).reshape((TSTEPS, SENSOR_BLOCKS, BLOCKS_PER))
    blocks = normal_values(streams_of[2], (SENSOR_BLOCKS, BLOCK_ROWS, BLOCKS_PER * BLOCK_COLS), 0.03, 0.18, ((0, 4),), jnp.float32)
    sensor_precision = jnp.clip(jnp.exp(math.log(4.0) - 2.7725887 * jax.random.uniform(streams_of[3], (SENSORS,), jnp.float32) ** level_of(streams_of[3], (SENSORS,), ((0, 4),), -0.2, 0.2)), 0.25, 4.0)
    transition = draw_transition(jax.random.fold_in(streams_of[8], 71), 0)
    process_precision = draw_process_precision(jax.random.fold_in(streams_of[8], 71), 0)
    prior_mean = normal_values(streams_of[6], (STATE,), 1.0, 6.0, (), jnp.float32)
    prior_precision = draw_prior_precision(jax.random.fold_in(streams_of[8], 71), 0)
    return {"observations": observations, "pattern": pattern, "blocks": blocks, "sensor_precision": sensor_precision, "transition": transition, "process_precision": process_precision, "prior_mean": prior_mean, "prior_precision": prior_precision}


def matmul(left, right):
    return jnp.dot(left, right, precision=lax.Precision.HIGHEST)

def dense_rows(pattern_now, blocks):
    groups, rows_blk, block_width = blocks.shape
    per_group = pattern_now.shape[1]
    columns = block_width // per_group
    block_ids = jnp.arange(STATE // columns, dtype=jnp.int32)
    onehot = (pattern_now[:, :, None] == block_ids[None, None, :]).astype(jnp.float32)
    pieces = blocks.reshape(groups, rows_blk, per_group, columns)
    placed = jnp.einsum('grkc,gkj->grjc', pieces, onehot, precision=lax.Precision.HIGHEST)
    return placed.reshape(groups * rows_blk, STATE)

def information(observed, pattern_now, blocks, sensor_precision):
    sensed = dense_rows(pattern_now, blocks)
    weighted = sensed * sensor_precision[:, None]
    return (matmul(sensed.T, weighted), matmul(observed, weighted))

def reference(observations, pattern, blocks, sensor_precision, transition, process_precision, prior_mean, prior_precision):
    identity = jnp.eye(STATE, dtype=jnp.float32)
    scaled_transition = matmul(process_precision, transition)
    matrix, vector = information(observations[0], pattern[0], blocks, sensor_precision)
    covariance = jnp.linalg.solve(prior_precision + matrix, identity)
    mean_now = matmul(covariance, vector + matmul(prior_precision, prior_mean))

    def advance(filtered, inputs):
        mean_prev, cov_prev = filtered
        observed, pattern_now = inputs
        matrix_now, vector_now = information(observed, pattern_now, blocks, sensor_precision)
        cov_step = jnp.linalg.solve(process_precision + matrix_now, identity)
        linear = matmul(cov_step, scaled_transition)
        mean_step = matmul(cov_step, vector_now)
        mixed_mat = matmul(matrix_now, cov_step)
        info_mat = matmul(transition.T, matmul(matrix_now - matmul(mixed_mat, matrix_now), transition))
        info_vec = matmul(vector_now - matmul(mixed_mat, vector_now), transition)
        coupled = identity + matmul(cov_prev, info_mat)
        moved_mean = jnp.linalg.solve(coupled, mean_prev + matmul(cov_prev, info_vec))
        moved_cov = jnp.linalg.solve(coupled, cov_prev)
        mean_new = matmul(linear, moved_mean) + mean_step
        cov_new = matmul(matmul(linear, moved_cov), linear.T) + cov_step
        return ((mean_new, cov_new), (mean_new, jnp.diagonal(cov_new)))
    final_item, outputs = lax.scan(advance, (mean_now, covariance), (observations[1:], pattern[1:]))
    means = jnp.concatenate([mean_now[None], outputs[0]], 0)
    variances = jnp.concatenate([jnp.diagonal(covariance)[None], outputs[1]], 0)
    return (means, variances)
```

```python
import functools

import jax
import jax.numpy as jnp
from jax import lax
from jax.experimental import pallas as pl
from jax.experimental.pallas import tpu as pltpu
from jax.sharding import PartitionSpec as P

def mm(a, b, prec=lax.Precision.HIGHEST, ta=False, tb=False):
    return lax.dot_general(a, b, (((0 if ta else 1,), (1 if tb else 0,)), ((), ())),
                           precision=prec, preferred_element_type=jnp.float32)

def pivots(mat, lanes, rows_in, first, width):
    size = mat.shape[0]
    cols = [jnp.broadcast_to(mat[:, first + i:first + i + 1], mat.shape) for i in range(width)]
    piv = [[cols[j][first + i:first + i + 1, :] for j in range(width)] for i in range(width)]
    rows = []
    for i in range(width):
        row = mat[first + i:first + i + 1, :]
        for j in range(width):
            row = jnp.where(lanes == first + j, 1.0 if i == j else 0.0, row)
        rows.append(row)
    def inv2(p):
        rdet = 1.0 / (p[0][0] * p[1][1] - p[0][1] * p[1][0])
        return [[p[1][1] * rdet, -p[0][1] * rdet], [-p[1][0] * rdet, p[0][0] * rdet]]
    def mul2(x, y):
        return [[x[i][0] * y[0][j] + x[i][1] * y[1][j] for j in range(2)] for i in range(2)]
    if width == 1:
        new = [rows[0] * (1.0 / piv[0][0])]
    elif width == 2:
        q = inv2(piv)
        new = [q[i][0] * rows[0] + q[i][1] * rows[1] for i in range(2)]
    else:
        a = [r[:2] for r in piv[:2]]; b = [r[2:] for r in piv[:2]]
        c = [r[:2] for r in piv[2:]]; d = [r[2:] for r in piv[2:]]
        ai = inv2(a)
        x = mul2(c, ai)
        xb = mul2(x, b)
        s = [[d[i][j] - xb[i][j] for j in range(2)] for i in range(2)]
        si = inv2(s)
        low = [rows[2 + i] - x[i][0] * rows[0] - x[i][1] * rows[1] for i in range(2)]
        bot = [si[i][0] * low[0] + si[i][1] * low[1] for i in range(2)]
        up = [rows[i] - b[i][0] * bot[0] - b[i][1] * bot[1] for i in range(2)]
        top = [ai[i][0] * up[0] + ai[i][1] * up[1] for i in range(2)]
        new = top + bot
    keep = jnp.where((lanes >= first) & (lanes < first + width), 0.0, mat)
    for i in range(width):
        keep = keep - cols[i] * new[i]
    for i in range(width):
        keep = jnp.where(rows_in == first + i, new[i], keep)
    return keep

def inv_small(mats, width=4):
    size = mats[0].shape[0]
    lanes = lax.broadcasted_iota(jnp.int32, (1, size), 1)
    rows_in = lax.broadcasted_iota(jnp.int32, (size, 1), 0)
    def body(_, ms):
        ms = list(ms)
        for first in range(0, 8, width):
            ms = [pivots(m, lanes, rows_in, first, width) for m in ms]
        out = []
        for m in ms:
            m = pltpu.roll(m, size - 8, 1)
            m = jnp.concatenate([m[8:], m[:8]], 0)
            out.append(m)
        return tuple(out)
    return list(lax.fori_loop(0, size // 8, body, tuple(mats)))

def inv_full(mats, width=4):
    h = mats[0].shape[0] // 2
    firsts = inv_small([m[:h, :h] for m in mats], width)
    right = [mm(f, m[:h, h:]) for f, m in zip(firsts, mats)]
    schur = [m[h:, h:] - mm(m[h:, :h], r) for m, r in zip(mats, right)]
    lasts = inv_small(schur, width)
    outs = []
    for f, r, l in zip(firsts, right, lasts):
        y = mm(r, l)
        top = jnp.concatenate([f + mm(y, r, tb=True), -y], 1)
        bot = jnp.concatenate([-y.T, l], 1)
        outs.append(jnp.concatenate([top, bot], 0))
    return outs


def join(earlier, later, inner, full=True):
    early_first, early_cross, early_last, early_h1, early_h2 = earlier
    late_first, late_cross, late_last, late_h1, late_h2 = later
    solved = mm(inner, late_cross)
    shift = mm(early_h2 + late_h1, inner)
    last = late_last - mm(late_cross, solved, ta=True)
    h2 = late_h2 - mm(shift, late_cross)
    if not full:
        return (None, None, last, None, h2)
    cross = -mm(early_cross, solved)
    first = early_first - mm(mm(early_cross, inner), early_cross, tb=True)
    h1 = early_h1 - mm(shift, early_cross, tb=True)
    return (first, cross, last, h1, h2)


def join_two(earlier, laters, full=True):
    inners = inv_full([e[2] + l[0] for e, l in zip(earlier, laters)])
    return [join(e, l, n, full) for e, l, n in zip(earlier, laters, inners)]


def pick(flag, yes, no):
    return tuple(jnp.where(flag, y, n) for y, n in zip(yes, no))


def save(ref, span):
    size = span[0].shape[0]
    for i in range(3):
        ref[i * size:(i + 1) * size] = span[i]
    ref[3 * size:3 * size + 1] = span[3]
    ref[3 * size + 1:3 * size + 2] = span[4]


def load(ref):
    size = ref.shape[1]
    return (ref[:size], ref[size:2 * size], ref[2 * size:3 * size], ref[3 * size:3 * size + 1], ref[3 * size + 1:3 * size + 2])


def local_kernel(axes, mats, vecs, trans, proc, prior, mean, own_ref, total_ref):
    first = lax.axis_index(axes[0]) == 0
    place = lax.axis_index(axes[1])
    process = proc[...]
    pulled = mm(trans[...], process, ta=True)
    back = mm(pulled, trans[...])
    zero = jnp.zeros((1, back.shape[0]), jnp.float32)

    def span(i):
        return (back, -pulled, process + mats[i], zero, vecs[i:i + 1])

    start = (
        jnp.zeros_like(back),
        jnp.zeros_like(back),
        prior[...] + mats[0],
        zero,
        vecs[0:1] + mm(mean[...], prior[...]),
    )
    zeroth = pick(first, start, span(0))
    left, right = join_two([zeroth, span(2)], [span(1), span(3)])
    total, third = join_two([left, left], [right, span(2)])
    own = pick(place == 0, zeroth, pick(place == 1, left, pick(place == 2, third, total)))
    save(own_ref, own)
    save(total_ref, total)


def level_kernel(axis, distance, got, own, total, own_ref, total_ref):
    has = lax.axis_index(axis) >= distance
    mine, whole, came = load(own), load(total), load(got)
    new_own, new_total = join_two([came, came], [mine, whole])
    save(own_ref, pick(has, new_own, mine))
    save(total_ref, pick(has, new_total, whole))


def last_kernel(axis, distance, got, own, mean_ref, var_ref):
    has = lax.axis_index(axis) >= distance
    mine, came = load(own), load(got)
    inner = inv_full([came[2] + mine[0]])[0]
    new = join(came, mine, inner, False)
    last = jnp.where(has, new[2], mine[2])
    vec = jnp.where(has, new[4], mine[4])
    cov = inv_full([last])[0]
    rows = lax.broadcasted_iota(jnp.int32, cov.shape, 0)
    columns = lax.broadcasted_iota(jnp.int32, cov.shape, 1)
    mean_ref[...] = mm(vec, cov)
    var_ref[...] = jnp.sum(jnp.where(rows == columns, cov, 0.0), axis=0, keepdims=True)


def call(kernel, outs, *args):
    return pl.pallas_call(
        kernel,
        out_shape=outs,
        in_specs=[pl.BlockSpec(memory_space=pltpu.VMEM)] * len(args),
        out_specs=[pl.BlockSpec(memory_space=pltpu.VMEM)] * len(outs),
        compiler_params=pltpu.CompilerParams(vmem_limit_bytes=40 << 20),
    )(*args)


def dense_rows(pattern_now, blocks, state_size):
    groups, rows_blk, block_width = blocks.shape
    per_group = pattern_now.shape[1]
    columns = block_width // per_group
    block_ids = jnp.arange(state_size // columns, dtype=jnp.int32)
    onehot = (pattern_now[:, :, None] == block_ids[None, None, :]).astype(jnp.float32)
    pieces = blocks.reshape(groups, rows_blk, per_group, columns)
    placed = jnp.einsum("grkc,gkj->grjc", pieces, onehot, precision=lax.Precision.HIGHEST)
    return placed.reshape(groups * rows_blk, state_size)


def information(inputs, blocks, sensor_precision, state_size):
    observed, pattern_now = inputs
    sensed = dense_rows(pattern_now, blocks, state_size)
    weighted = sensed * sensor_precision[:, None]
    return (mm(sensed.T, weighted), jnp.dot(observed, weighted, precision=lax.Precision.HIGHEST))


def shards(observations, pattern, blocks, sensor_precision, transition, process_precision, prior_mean, prior_precision):
    size = transition.shape[0]
    matrix_parts, vector_parts = jax.vmap(
        functools.partial(information, blocks=blocks, sensor_precision=sensor_precision, state_size=size)
    )((observations, pattern))
    matrices, vectors = lax.psum((matrix_parts, vector_parts), "sens")
    span = jax.ShapeDtypeStruct((3 * size + 8, size), jnp.float32)
    own, total = call(
        functools.partial(local_kernel, ("tm", "sens")),
        [span, span],
        matrices, vectors, transition, process_precision, prior_precision, prior_mean[None],
    )
    turns = lax.axis_size("tm")
    distance = 1
    while True:
        got = lax.ppermute(total, "tm", [(i, i + distance) for i in range(turns - distance)])
        if 2 * distance >= turns:
            break
        own, total = call(functools.partial(level_kernel, "tm", distance), [span, span], got, own, total)
        distance *= 2
    row = jax.ShapeDtypeStruct((1, size), jnp.float32)
    return tuple(call(functools.partial(last_kernel, "tm", distance), [row, row], got, own))


def solution(mesh):
    placed = (P("tm", "sens"), P("tm", "sens", None), P("sens", None, None), P("sens"), P(), P(), P(), P())
    return jax.shard_map(
        shards,
        mesh=mesh,
        in_specs=placed,
        out_specs=(P(("tm", "sens"), None), P(("tm", "sens"), None)),
        check_vma=False,
    )
```

```python
import functools

import jax
import jax.numpy as jnp
from jax import lax
from jax.experimental import pallas as pl
from jax.experimental.pallas import tpu as pltpu
from jax.sharding import PartitionSpec as P

def mm(a, b, prec=lax.Precision.HIGHEST, ta=False, tb=False):
    return lax.dot_general(a, b, (((0 if ta else 1,), (1 if tb else 0,)), ((), ())),
                           precision=prec, preferred_element_type=jnp.float32)

def pivots(mat, lanes, rows_in, first, width):
    size = mat.shape[0]
    cols = [jnp.broadcast_to(mat[:, first + i:first + i + 1], mat.shape) for i in range(width)]
    piv = [[cols[j][first + i:first + i + 1, :] for j in range(width)] for i in range(width)]
    rows = []
    for i in range(width):
        row = mat[first + i:first + i + 1, :]
        for j in range(width):
            row = jnp.where(lanes == first + j, 1.0 if i == j else 0.0, row)
        rows.append(row)
    def inv2(p):
        rdet = 1.0 / (p[0][0] * p[1][1] - p[0][1] * p[1][0])
        return [[p[1][1] * rdet, -p[0][1] * rdet], [-p[1][0] * rdet, p[0][0] * rdet]]
    def mul2(x, y):
        return [[x[i][0] * y[0][j] + x[i][1] * y[1][j] for j in range(2)] for i in range(2)]
    if width == 1:
        new = [rows[0] * (1.0 / piv[0][0])]
    elif width == 2:
        q = inv2(piv)
        new = [q[i][0] * rows[0] + q[i][1] * rows[1] for i in range(2)]
    else:
        a = [r[:2] for r in piv[:2]]; b = [r[2:] for r in piv[:2]]
        c = [r[:2] for r in piv[2:]]; d = [r[2:] for r in piv[2:]]
        ai = inv2(a)
        x = mul2(c, ai)
        xb = mul2(x, b)
        s = [[d[i][j] - xb[i][j] for j in range(2)] for i in range(2)]
        si = inv2(s)
        low = [rows[2 + i] - x[i][0] * rows[0] - x[i][1] * rows[1] for i in range(2)]
        bot = [si[i][0] * low[0] + si[i][1] * low[1] for i in range(2)]
        up = [rows[i] - b[i][0] * bot[0] - b[i][1] * bot[1] for i in range(2)]
        top = [ai[i][0] * up[0] + ai[i][1] * up[1] for i in range(2)]
        new = top + bot
    keep = jnp.where((lanes >= first) & (lanes < first + width), 0.0, mat)
    for i in range(width):
        keep = keep - cols[i] * new[i]
    for i in range(width):
        keep = jnp.where(rows_in == first + i, new[i], keep)
    return keep

def inv_small(mats, width=4):
    size = mats[0].shape[0]
    lanes = lax.broadcasted_iota(jnp.int32, (1, size), 1)
    rows_in = lax.broadcasted_iota(jnp.int32, (size, 1), 0)
    def body(_, ms):
        ms = list(ms)
        for first in range(0, 8, width):
            ms = [pivots(m, lanes, rows_in, first, width) for m in ms]
        out = []
        for m in ms:
            m = pltpu.roll(m, size - 8, 1)
            m = jnp.concatenate([m[8:], m[:8]], 0)
            out.append(m)
        return tuple(out)
    return list(lax.fori_loop(0, size // 8, body, tuple(mats)))

def inv_full(mats, width=4):
    h = mats[0].shape[0] // 2
    firsts = inv_small([m[:h, :h] for m in mats], width)
    right = [mm(f, m[:h, h:]) for f, m in zip(firsts, mats)]
    schur = [m[h:, h:] - mm(m[h:, :h], r) for m, r in zip(mats, right)]
    lasts = inv_small(schur, width)
    outs = []
    for f, r, l in zip(firsts, right, lasts):
        y = mm(r, l)
        top = jnp.concatenate([f + mm(y, r, tb=True), -y], 1)
        bot = jnp.concatenate([-y.T, l], 1)
        outs.append(jnp.concatenate([top, bot], 0))
    return outs


def close(earlier, later, inner):
    solved = mm(inner, later["K"])
    shift = mm(earlier["h2"] + later["h1"], inner)
    last = later["P22"] - mm(later["K"], solved, ta=True)
    return solved, shift, last, later["h2"] - mm(shift, later["K"])


def join(earlier, later, inner):
    solved, shift, last, h2 = close(earlier, later, inner)
    cross = -mm(earlier["K"], solved)
    first = earlier["P11"] - mm(mm(earlier["K"], inner), earlier["K"], tb=True)
    h1 = earlier["h1"] - mm(shift, earlier["K"], tb=True)
    return {"P11": first, "K": cross, "P22": last, "h1": h1, "h2": h2}


def pick(flag, yes, no):
    return {name: jnp.where(flag, yes[name], no[name]) for name in yes}


class Span:
    def __init__(self, ref, size):
        self.ref = ref
        self.at = {
            "P22": (0, size), "h2": (size, 1), "h1": (size + 8, 1),
            "P11": (size + 16, size), "K": (2 * size + 16, size),
        }
        self.parts = ((0, size + 16), (size + 16, 2 * size))

    def __getitem__(self, name):
        start, count = self.at[name]
        return self.ref[start:start + count]

    def keep(self, span):
        for name, (start, count) in self.at.items():
            self.ref[start:start + count] = span[name]

    def part(self, i):
        start, count = self.parts[i]
        return self.ref.at[start:start + count]


MESH = pl.DeviceIdType.MESH


def filter_kernel(turns, planes, distances, *refs):
    (obs, wide, blocks, weights, trans, proc, mean, prior, mean_ref, var_ref,
     gram, held, turned, sights, vectors, mats, own_buf, totals, came,
     gram_send, gram_recv, side_send, side_recv, sight_send, sight_recv, vec_send, vec_recv,
     span_send, span_recv) = refs
    steps = obs.shape[0]
    size = trans.shape[0]
    groups, rows_blk, width = blocks.shape
    half = width // 2
    pairs = groups // 2
    mine_pairs = pairs // 2
    tm = lax.axis_index("tm")
    plane = lax.axis_index("sens")
    core = lax.rem(tm, 2)
    other = tm + 1 - 2 * core

    def peer(shift):
        return (tm, lax.rem(plane + shift, planes))

    barrier = pltpu.get_barrier_semaphore()

    def greet(device):
        pl.semaphore_signal(barrier, inc=1, device_id=device, device_id_type=MESH)

    for shift in range(1, planes):
        greet(peer(shift))
    greet((other, plane))
    for distance in distances:
        greet((lax.rem(tm + distance, turns), plane))
        greet((lax.rem(tm + turns - distance, turns), plane))

    lanes = lax.broadcasted_iota(jnp.int32, (1, width), 1)
    left = lanes < half

    for i in range(mine_pairs):
        packed = []
        for j in range(2):
            g = (core * mine_pairs + i) * 2 + j
            block = blocks[g]
            packed.append(mm(block.T * weights[g], block))
        slot = core * mine_pairs + i
        gram[0, slot, :half] = packed[0][:half]
        gram[0, slot, half:2 * half] = packed[1][:half]
        gram[0, slot, 2 * half:] = jnp.concatenate([packed[0][half:, half:], packed[1][half:, half:]], 1)

    sights[0] = wide[...]
    sums = [[jnp.zeros((1, width), jnp.float32) for _ in range(size // width)] for _ in range(steps)]

    def targets(tile):
        return jnp.where(left, 2.0 * tile, 2.0 * tile + 1.0)

    for g in range(groups):
        seen = mm(obs[:, g * rows_blk:(g + 1) * rows_blk] * weights[g], blocks[g])
        swapped = pltpu.roll(jnp.concatenate([seen, seen], 0), half, 1)
        for t in range(steps):
            first = wide[t, g, 0:1]
            second = wide[t, g, 1:2]
            straight = jnp.where(left, first, second)
            crossed = jnp.where(left, second, first)
            for tile in range(size // width):
                sums[t][tile] += jnp.where(straight == targets(tile), seen[t:t + 1], 0.0) + jnp.where(crossed == targets(tile), swapped[t:t + 1], 0.0)
    vectors[0] = jnp.zeros(vectors.shape[1:], jnp.float32)
    for t in range(steps):
        vectors[0, t:t + 1] = jnp.concatenate(sums[t], 1)

    pl.semaphore_wait(barrier, planes + 2 * len(distances))

    def share(slot):
        return gram.at[slot, pl.ds(core * mine_pairs, mine_pairs)]

    def remote(source, target, send, recv, device):
        return pltpu.make_async_remote_copy(
            src_ref=source, dst_ref=target, send_sem=send, recv_sem=recv, device_id=device, device_id_type=MESH
        )

    out = []
    for shift in range(1, planes):
        out.append(remote(share(0), share(shift), gram_send.at[shift], gram_recv.at[shift], peer(shift)))
        out.append(remote(vectors.at[0], vectors.at[shift], vec_send.at[shift], vec_recv.at[shift], peer(shift)))
        out.append(remote(sights.at[0], sights.at[shift], sight_send.at[shift], sight_recv.at[shift], peer(shift)))
    side = [remote(share(slot), share(slot), side_send.at[slot], side_recv.at[slot], (other, plane)) for slot in range(planes)]
    for copy in out:
        copy.start()
    side[0].start()

    process = proc[...]
    pulled = mm(trans[...], process, ta=True)
    back = mm(pulled, trans[...])
    start_vec = mm(mean[...], prior[...])

    for t in range(steps):
        mats[t] = jnp.zeros((size, size), jnp.float32)

    for slot in range(planes):
        if slot:
            for copy in out[3 * slot - 3:3 * slot]:
                copy.wait_recv()
            side[slot].start()
    for slot in range(planes):
        side[slot].wait_recv()

        def unpack(g, _):
            pair, j = g // 2, g % 2
            top = gram[slot, pair, pl.ds(pl.multiple_of(j * half, half), half)]
            rest = gram[slot, pair, 2 * half:]
            corner = jnp.where(j == 0, rest, pltpu.roll(rest, half, 1))
            cross = jnp.concatenate([top, top], 0).T[half:, :half]
            low = jnp.concatenate([cross, corner[:, :half]], 1)
            full = jnp.concatenate([top, low], 0)
            held[slot * groups + g] = full
            turned[slot * groups + g] = pltpu.roll(full, half, 1)
            return 0

        lax.fori_loop(0, groups, unpack, 0)

    for t in range(steps):
        for tile in range(size // width):
            def place(g, sums):
                slot, local = g // groups, g % groups
                first = sights[slot, t, local, 0:1]
                second = sights[slot, t, local, 1:2]
                straight = jnp.where(left, first, second) == targets(tile)
                crossed = jnp.where(left, second, first) == targets(tile)
                put = jnp.where(straight, held[g], jnp.where(crossed, turned[g], 0.0))
                return tuple(
                    total + jnp.where(first == 1.0 * j, put[:half], jnp.where(second == 1.0 * j, put[half:], 0.0))
                    for j, total in enumerate(sums)
                )

            blocks_sum = lax.fori_loop(
                0, planes * groups, place, tuple(jnp.zeros((half, width), jnp.float32) for _ in range(size // half))
            )
            for j in range(size // half):
                mats[t, j * half:(j + 1) * half, tile * width:(tile + 1) * width] = blocks_sum[j]
    vecs = vectors[0]
    for slot in range(1, planes):
        vecs = vecs + vectors[slot]

    zero = jnp.zeros((1, size), jnp.float32)
    first_turn = tm == 0

    def span(i):
        return {"P11": back, "K": -pulled, "P22": process + mats[i], "h1": zero, "h2": vecs[i:i + 1]}

    start = {
        "P11": jnp.zeros_like(back), "K": jnp.zeros_like(back), "P22": prior[...] + mats[0],
        "h1": zero, "h2": vecs[0:1] + start_vec,
    }
    zeroth = pick(first_turn, start, span(0))
    inners = inv_full([zeroth["P22"] + back, span(2)["P22"] + back])
    pair_low = join(zeroth, span(1), inners[0])
    pair_high = join(span(2), span(3), inners[1])
    inners = inv_full([pair_low["P22"] + pair_high["P11"], pair_low["P22"] + back])
    whole = join(pair_low, pair_high, inners[0])
    third = join(pair_low, span(2), inners[1])
    own = Span(own_buf, size)
    own.keep(pick(plane == 0, zeroth, pick(plane == 1, pair_low, pick(plane == 2, third, whole))))
    blank = jnp.zeros((16, size), jnp.float32)
    for level in range(len(distances)):
        totals[level, size:size + 16] = blank
    Span(totals.at[0], size).keep(whole)

    for level, distance in enumerate(distances):
        final = level == len(distances) - 1
        total = Span(totals.at[level], size)
        got = Span(came.at[level], size)
        count = 1 if final else 2
        copies = [
            remote(total.part(i), got.part(i), span_send.at[2 * level + i], span_recv.at[2 * level + i], (tm + distance, plane))
            for i in range(count)
        ]

        @pl.when(tm + distance < turns)
        def _():
            for copy in copies:
                copy.start()

        @pl.when(tm >= distance)
        def _():
            copies[0].wait_recv()
            if final:
                inner = inv_full([got["P22"] + own["P11"]])[0]
                _, _, last, h2 = close(got, own, inner)
                own.ref[0:size] = last
                own.ref[size:size + 1] = h2
            else:
                inners = inv_full([got["P22"] + own["P11"], got["P22"] + total["P11"]])
                copies[1].wait_recv()
                Span(totals.at[level + 1], size).keep(join(got, total, inners[1]))
                own.keep(join(got, own, inners[0]))

        if not final:
            @pl.when(tm < distance)
            def _():
                Span(totals.at[level + 1], size).keep(total)

        @pl.when(tm + distance < turns)
        def _():
            for copy in copies:
                copy.wait_send()

    cov = inv_full([own["P22"]])[0]
    rows = lax.broadcasted_iota(jnp.int32, cov.shape, 0)
    columns = lax.broadcasted_iota(jnp.int32, cov.shape, 1)
    mean_ref[...] = mm(own["h2"], cov)
    var_ref[...] = jnp.sum(jnp.where(rows == columns, cov, 0.0), axis=0, keepdims=True)
    for copy in out + side:
        copy.wait_send()


def shards(observations, pattern, blocks, sensor_precision, transition, process_precision, prior_mean, prior_precision):
    size = transition.shape[0]
    groups, rows_blk, width = blocks.shape
    steps = observations.shape[0]
    turns, planes = lax.axis_size("tm"), lax.axis_size("sens")
    distances = []
    while 2 ** len(distances) < turns:
        distances.append(2 ** len(distances))
    levels = len(distances)
    wide = jnp.broadcast_to(pattern.astype(jnp.float32)[..., None], pattern.shape + (width,))
    wide = jnp.pad(wide, ((0, 0), (0, 0), (0, 8 - pattern.shape[2]), (0, 0)))
    row = jax.ShapeDtypeStruct((1, size), jnp.float32)
    span = (3 * size + 16, size)
    dma = pltpu.SemaphoreType.DMA
    args = (
        observations, wide, blocks, sensor_precision.reshape(groups, 1, rows_blk), transition,
        process_precision, prior_mean[None], prior_precision,
    )
    return tuple(pl.pallas_call(
        functools.partial(filter_kernel, turns, planes, distances),
        out_shape=[row, row],
        in_specs=[pl.BlockSpec(memory_space=pltpu.VMEM)] * len(args),
        out_specs=[pl.BlockSpec(memory_space=pltpu.VMEM)] * 2,
        scratch_shapes=[
            pltpu.VMEM((planes, groups // 2, 3 * width // 2, width), jnp.float32),
            pltpu.VMEM((planes * groups, width, width), jnp.float32),
            pltpu.VMEM((planes * groups, width, width), jnp.float32),
            pltpu.VMEM((planes,) + wide.shape, jnp.float32),
            pltpu.VMEM((planes, 8, size), jnp.float32),
            pltpu.VMEM((steps, size, size), jnp.float32),
            pltpu.VMEM(span, jnp.float32),
            pltpu.VMEM((levels,) + span, jnp.float32),
            pltpu.VMEM((levels,) + span, jnp.float32),
            dma((planes,)), dma((planes,)), dma((planes,)), dma((planes,)), dma((planes,)), dma((planes,)),
            dma((planes,)), dma((planes,)), dma((2 * levels,)), dma((2 * levels,)),
        ],
        compiler_params=pltpu.CompilerParams(collective_id=0, has_side_effects=True, vmem_limit_bytes=44 << 20),
    )(*args))


def solution(mesh):
    placed = (P("tm", "sens"), P("tm", "sens", None), P("sens", None, None), P("sens"), P(), P(), P(), P())
    return jax.shard_map(
        shards,
        mesh=mesh,
        in_specs=placed,
        out_specs=(P(("tm", "sens"), None), P(("tm", "sens"), None)),
        check_vma=False,
    )
```

```python
import functools

import jax
import jax.numpy as jnp
from jax import lax
from jax.experimental import pallas as pl
from jax.experimental.pallas import tpu as pltpu
from jax.sharding import PartitionSpec as P

def mm(a, b, prec=lax.Precision.HIGHEST, ta=False, tb=False):
    return lax.dot_general(a, b, (((0 if ta else 1,), (1 if tb else 0,)), ((), ())),
                           precision=prec, preferred_element_type=jnp.float32)

def pivots(mat, lanes, rows_in, first, width):
    size = mat.shape[0]
    cols = [jnp.broadcast_to(mat[:, first + i:first + i + 1], mat.shape) for i in range(width)]
    piv = [[cols[j][first + i:first + i + 1, :] for j in range(width)] for i in range(width)]
    rows = []
    for i in range(width):
        row = mat[first + i:first + i + 1, :]
        for j in range(width):
            row = jnp.where(lanes == first + j, 1.0 if i == j else 0.0, row)
        rows.append(row)
    def inv2(p):
        rdet = 1.0 / (p[0][0] * p[1][1] - p[0][1] * p[1][0])
        return [[p[1][1] * rdet, -p[0][1] * rdet], [-p[1][0] * rdet, p[0][0] * rdet]]
    def mul2(x, y):
        return [[x[i][0] * y[0][j] + x[i][1] * y[1][j] for j in range(2)] for i in range(2)]
    if width == 1:
        new = [rows[0] * (1.0 / piv[0][0])]
    elif width == 2:
        q = inv2(piv)
        new = [q[i][0] * rows[0] + q[i][1] * rows[1] for i in range(2)]
    else:
        a = [r[:2] for r in piv[:2]]; b = [r[2:] for r in piv[:2]]
        c = [r[:2] for r in piv[2:]]; d = [r[2:] for r in piv[2:]]
        ai = inv2(a)
        x = mul2(c, ai)
        xb = mul2(x, b)
        s = [[d[i][j] - xb[i][j] for j in range(2)] for i in range(2)]
        si = inv2(s)
        low = [rows[2 + i] - x[i][0] * rows[0] - x[i][1] * rows[1] for i in range(2)]
        bot = [si[i][0] * low[0] + si[i][1] * low[1] for i in range(2)]
        up = [rows[i] - b[i][0] * bot[0] - b[i][1] * bot[1] for i in range(2)]
        top = [ai[i][0] * up[0] + ai[i][1] * up[1] for i in range(2)]
        new = top + bot
    keep = jnp.where((lanes >= first) & (lanes < first + width), 0.0, mat)
    for i in range(width):
        keep = keep - cols[i] * new[i]
    for i in range(width):
        keep = jnp.where(rows_in == first + i, new[i], keep)
    return keep

def inv_small(mats, width=4, chunk=32):
    size = mats[0].shape[0]
    lanes = lax.broadcasted_iota(jnp.int32, (1, size), 1)
    rows_in = lax.broadcasted_iota(jnp.int32, (size, 1), 0)
    def body(_, ms):
        ms = list(ms)
        for first in range(0, chunk, width):
            ms = [pivots(m, lanes, rows_in, first, width) for m in ms]
        out = []
        for m in ms:
            m = pltpu.roll(m, size - chunk, 1)
            m = jnp.concatenate([m[chunk:], m[:chunk]], 0)
            out.append(m)
        return tuple(out)
    return list(lax.fori_loop(0, size // chunk, body, tuple(mats)))

def inv_full(mats, width=4):
    h = mats[0].shape[0] // 2
    firsts = inv_small([m[:h, :h] for m in mats], width)
    right = [mm(f, m[:h, h:]) for f, m in zip(firsts, mats)]
    schur = [m[h:, h:] - mm(m[h:, :h], r) for m, r in zip(mats, right)]
    lasts = inv_small(schur, width)
    outs = []
    for f, r, l in zip(firsts, right, lasts):
        y = mm(r, l)
        top = jnp.concatenate([f + mm(y, r, tb=True), -y], 1)
        bot = jnp.concatenate([-y.T, l], 1)
        outs.append(jnp.concatenate([top, bot], 0))
    return outs


def close(earlier, later, inner):
    solved = mm(inner, later["K"])
    shift = mm(earlier["h2"] + later["h1"], inner)
    last = later["P22"] - mm(later["K"], solved, ta=True)
    return solved, shift, last, later["h2"] - mm(shift, later["K"])


def join(earlier, later, inner):
    solved, shift, last, h2 = close(earlier, later, inner)
    cross = -mm(earlier["K"], solved)
    first = earlier["P11"] - mm(mm(earlier["K"], inner), earlier["K"], tb=True)
    h1 = earlier["h1"] - mm(shift, earlier["K"], tb=True)
    return {"P11": first, "K": cross, "P22": last, "h1": h1, "h2": h2}


def pick(flag, yes, no):
    return {name: jnp.where(flag, yes[name], no[name]) for name in yes}


class Span:
    def __init__(self, ref, size):
        self.ref = ref
        self.at = {
            "P22": (0, size), "h2": (size, 1), "h1": (size + 8, 1),
            "P11": (size + 16, size), "K": (2 * size + 16, size),
        }
        self.parts = ((0, size + 16), (size + 16, 2 * size))

    def __getitem__(self, name):
        start, count = self.at[name]
        return self.ref[start:start + count]

    def keep(self, span):
        for name, (start, count) in self.at.items():
            self.ref[start:start + count] = span[name]

    def part(self, i):
        start, count = self.parts[i]
        return self.ref.at[start:start + count]


MESH = pl.DeviceIdType.MESH


def filter_kernel(turns, planes, distances, *refs):
    (obs, wide, blocks, weights, trans, proc, mean, prior, mean_ref, var_ref,
     gram, held, turned, sights, vectors, mats, own_buf, totals, came,
     gram_send, gram_recv, side_send, side_recv, sight_send, sight_recv, vec_send, vec_recv,
     span_send, span_recv) = refs
    steps = obs.shape[0]
    size = trans.shape[0]
    groups, rows_blk, width = blocks.shape
    half = width // 2
    pairs = groups // 2
    mine_pairs = pairs // 2
    tm = lax.axis_index("tm")
    plane = lax.axis_index("sens")
    core = lax.rem(tm, 2)
    other = tm + 1 - 2 * core

    def peer(shift):
        return (tm, lax.rem(plane + shift, planes))

    barrier = pltpu.get_barrier_semaphore()

    def greet(device):
        pl.semaphore_signal(barrier, inc=1, device_id=device, device_id_type=MESH)

    for shift in range(1, planes):
        greet(peer(shift))
    greet((other, plane))
    for distance in distances:
        greet((lax.rem(tm + distance, turns), plane))
        greet((lax.rem(tm + turns - distance, turns), plane))

    lanes = lax.broadcasted_iota(jnp.int32, (1, width), 1)
    left = lanes < half

    for i in range(mine_pairs):
        packed = []
        for j in range(2):
            g = (core * mine_pairs + i) * 2 + j
            block = blocks[g]
            packed.append(mm(block.T * weights[g], block))
        slot = core * mine_pairs + i
        gram[0, slot, :half] = packed[0][:half]
        gram[0, slot, half:2 * half] = packed[1][:half]
        gram[0, slot, 2 * half:] = jnp.concatenate([packed[0][half:, half:], packed[1][half:, half:]], 1)

    sights[0] = wide[...]
    sums = [[jnp.zeros((1, width), jnp.float32) for _ in range(size // width)] for _ in range(steps)]

    def targets(tile):
        return jnp.where(left, 2.0 * tile, 2.0 * tile + 1.0)

    for g in range(groups):
        seen = mm(obs[:, g * rows_blk:(g + 1) * rows_blk] * weights[g], blocks[g])
        swapped = pltpu.roll(jnp.concatenate([seen, seen], 0), half, 1)
        for t in range(steps):
            first = wide[t, g, 0:1]
            second = wide[t, g, 1:2]
            straight = jnp.where(left, first, second)
            crossed = jnp.where(left, second, first)
            for tile in range(size // width):
                sums[t][tile] += jnp.where(straight == targets(tile), seen[t:t + 1], 0.0) + jnp.where(crossed == targets(tile), swapped[t:t + 1], 0.0)
    vectors[0] = jnp.zeros(vectors.shape[1:], jnp.float32)
    for t in range(steps):
        vectors[0, t:t + 1] = jnp.concatenate(sums[t], 1)

    pl.semaphore_wait(barrier, planes + 2 * len(distances))

    def share(slot):
        return gram.at[slot, pl.ds(core * mine_pairs, mine_pairs)]

    def remote(source, target, send, recv, device):
        return pltpu.make_async_remote_copy(
            src_ref=source, dst_ref=target, send_sem=send, recv_sem=recv, device_id=device, device_id_type=MESH
        )

    out = []
    for shift in range(1, planes):
        out.append(remote(share(0), share(shift), gram_send.at[shift], gram_recv.at[shift], peer(shift)))
        out.append(remote(vectors.at[0], vectors.at[shift], vec_send.at[shift], vec_recv.at[shift], peer(shift)))
        out.append(remote(sights.at[0], sights.at[shift], sight_send.at[shift], sight_recv.at[shift], peer(shift)))
    side = [remote(share(slot), share(slot), side_send.at[slot], side_recv.at[slot], (other, plane)) for slot in range(planes)]
    for copy in out:
        copy.start()
    side[0].start()

    process = proc[...]
    pulled = mm(trans[...], process, ta=True)
    back = mm(pulled, trans[...])
    start_vec = mm(mean[...], prior[...])

    for t in range(steps):
        mats[t] = jnp.zeros((size, size), jnp.float32)

    for slot in range(planes):
        if slot:
            for copy in out[3 * slot - 3:3 * slot]:
                copy.wait_recv()
            side[slot].start()
    for slot in range(planes):
        side[slot].wait_recv()

        def unpack(g, _):
            pair, j = g // 2, g % 2
            top = gram[slot, pair, pl.ds(pl.multiple_of(j * half, half), half)]
            rest = gram[slot, pair, 2 * half:]
            corner = jnp.where(j == 0, rest, pltpu.roll(rest, half, 1))
            cross = jnp.concatenate([top, top], 0).T[half:, :half]
            low = jnp.concatenate([cross, corner[:, :half]], 1)
            full = jnp.concatenate([top, low], 0)
            held[slot * groups + g] = full
            turned[slot * groups + g] = pltpu.roll(full, half, 1)
            return 0

        lax.fori_loop(0, groups, unpack, 0)

    for t in range(steps):
        for tile in range(size // width):
            def place(g, sums):
                slot, local = g // groups, g % groups
                first = sights[slot, t, local, 0:1]
                second = sights[slot, t, local, 1:2]
                straight = jnp.where(left, first, second) == targets(tile)
                crossed = jnp.where(left, second, first) == targets(tile)
                put = jnp.where(straight, held[g], jnp.where(crossed, turned[g], 0.0))
                return tuple(
                    total + jnp.where(first == 1.0 * j, put[:half], jnp.where(second == 1.0 * j, put[half:], 0.0))
                    for j, total in enumerate(sums)
                )

            blocks_sum = lax.fori_loop(
                0, planes * groups, place, tuple(jnp.zeros((half, width), jnp.float32) for _ in range(size // half))
            )
            for j in range(size // half):
                mats[t, j * half:(j + 1) * half, tile * width:(tile + 1) * width] = blocks_sum[j]
    vecs = vectors[0]
    for slot in range(1, planes):
        vecs = vecs + vectors[slot]

    zero = jnp.zeros((1, size), jnp.float32)
    first_turn = tm == 0

    def span(i):
        return {"P11": back, "K": -pulled, "P22": process + mats[i], "h1": zero, "h2": vecs[i:i + 1]}

    start = {
        "P11": jnp.zeros_like(back), "K": jnp.zeros_like(back), "P22": prior[...] + mats[0],
        "h1": zero, "h2": vecs[0:1] + start_vec,
    }
    zeroth = pick(first_turn, start, span(0))
    inners = inv_full([zeroth["P22"] + back, span(2)["P22"] + back])
    pair_low = join(zeroth, span(1), inners[0])
    pair_high = join(span(2), span(3), inners[1])
    inners = inv_full([pair_low["P22"] + pair_high["P11"], pair_low["P22"] + back])
    whole = join(pair_low, pair_high, inners[0])
    third = join(pair_low, span(2), inners[1])
    blank = jnp.zeros((16, size), jnp.float32)
    for level in range(len(distances)):
        totals[level, size:size + 16] = blank
    Span(totals.at[0], size).keep(whole)

    def copies_of(level):
        total, got = Span(totals.at[level], size), Span(came.at[level], size)
        return [
            remote(
                total.part(i), got.part(i), span_send.at[2 * level + i], span_recv.at[2 * level + i],
                (tm + distances[level], plane),
            )
            for i in range(1 if level == len(distances) - 1 else 2)
        ]

    def send(level):
        @pl.when(tm + distances[level] < turns)
        def _():
            for copy in copies_of(level):
                copy.start()

    send(0)
    own = Span(own_buf, size)
    own.keep(pick(plane == 0, zeroth, pick(plane == 1, pair_low, pick(plane == 2, third, whole))))

    for level, distance in enumerate(distances):
        final = level == len(distances) - 1
        total = Span(totals.at[level], size)
        got = Span(came.at[level], size)
        copies = copies_of(level)

        @pl.when(tm >= distance)
        def _():
            copies[0].wait_recv()
            if final:
                inner = inv_full([got["P22"] + own["P11"]])[0]
                _, _, last, h2 = close(got, own, inner)
                own.ref[0:size] = last
                own.ref[size:size + 1] = h2
            else:
                inners = inv_full([got["P22"] + own["P11"], got["P22"] + total["P11"]])
                copies[1].wait_recv()
                Span(totals.at[level + 1], size).keep(join(got, total, inners[1]))
                send(level + 1)
                own.keep(join(got, own, inners[0]))

        if not final:
            @pl.when(tm < distance)
            def _():
                Span(totals.at[level + 1], size).keep(total)
                send(level + 1)

        @pl.when(tm + distance < turns)
        def _():
            for copy in copies:
                copy.wait_send()

    cov = inv_full([own["P22"]])[0]
    rows = lax.broadcasted_iota(jnp.int32, cov.shape, 0)
    columns = lax.broadcasted_iota(jnp.int32, cov.shape, 1)
    mean_ref[...] = mm(own["h2"], cov)
    var_ref[...] = jnp.sum(jnp.where(rows == columns, cov, 0.0), axis=0, keepdims=True)
    for copy in out + side:
        copy.wait_send()


def shards(observations, pattern, blocks, sensor_precision, transition, process_precision, prior_mean, prior_precision):
    size = transition.shape[0]
    groups, rows_blk, width = blocks.shape
    steps = observations.shape[0]
    turns, planes = lax.axis_size("tm"), lax.axis_size("sens")
    distances = []
    while 2 ** len(distances) < turns:
        distances.append(2 ** len(distances))
    levels = len(distances)
    wide = jnp.broadcast_to(pattern.astype(jnp.float32)[..., None], pattern.shape + (width,))
    wide = jnp.pad(wide, ((0, 0), (0, 0), (0, 8 - pattern.shape[2]), (0, 0)))
    row = jax.ShapeDtypeStruct((1, size), jnp.float32)
    span = (3 * size + 16, size)
    dma = pltpu.SemaphoreType.DMA
    args = (
        observations, wide, blocks, sensor_precision.reshape(groups, 1, rows_blk), transition,
        process_precision, prior_mean[None], prior_precision,
    )
    return tuple(pl.pallas_call(
        functools.partial(filter_kernel, turns, planes, distances),
        out_shape=[row, row],
        in_specs=[pl.BlockSpec(memory_space=pltpu.VMEM)] * len(args),
        out_specs=[pl.BlockSpec(memory_space=pltpu.VMEM)] * 2,
        scratch_shapes=[
            pltpu.VMEM((planes, groups // 2, 3 * width // 2, width), jnp.float32),
            pltpu.VMEM((planes * groups, width, width), jnp.float32),
            pltpu.VMEM((planes * groups, width, width), jnp.float32),
            pltpu.VMEM((planes,) + wide.shape, jnp.float32),
            pltpu.VMEM((planes, 8, size), jnp.float32),
            pltpu.VMEM((steps, size, size), jnp.float32),
            pltpu.VMEM(span, jnp.float32),
            pltpu.VMEM((levels,) + span, jnp.float32),
            pltpu.VMEM((levels,) + span, jnp.float32),
            dma((planes,)), dma((planes,)), dma((planes,)), dma((planes,)), dma((planes,)), dma((planes,)),
            dma((planes,)), dma((planes,)), dma((2 * levels,)), dma((2 * levels,)),
        ],
        compiler_params=pltpu.CompilerParams(collective_id=0, has_side_effects=True, vmem_limit_bytes=44 << 20),
    )(*args))


def solution(mesh):
    placed = (P("tm", "sens"), P("tm", "sens", None), P("sens", None, None), P("sens"), P(), P(), P(), P())
    return jax.shard_map(
        shards,
        mesh=mesh,
        in_specs=placed,
        out_specs=(P(("tm", "sens"), None), P(("tm", "sens"), None)),
        check_vma=False,
    )
```
